512 devices in a mesh: ctx: 64 (over z, x, core), tp: 8 (over y).
Axes of the slice: x: 4, y: 8, z: 8, core: 2. Of those that a mesh axis runs over, the one named last changes fastest.
Arguments:
- queries: bfloat16 [8192, 64, 576], P('ctx', 'tp'), may hold values from -96 to 96
- latent_cache: bfloat16 [16, 8192, 576], P(None, ('ctx', 'tp')), may hold values from -16 to 16
- key_segments: int32 [1024, 128], replicated, may hold values from 0 to 2, as said below
- block_lists: int32 [64, 16], P('ctx'), may hold values from 0 to 1023, as said below
- value_up: bfloat16 [64, 512, 128], P('tp'), may hold values from -1 to 1
Outputs:
- attended: bfloat16 [8192, 8192], P('ctx', 'tp')
The draws below stay inside these ranges and needn't reach their ends.
Inputs may be any that keep to these rules, and one draw needn't show every extreme that they name: `block_lists`: row b lists 16 different blocks; its first entry is (15) * 64 + b, the block of query block b itself, and the others lie before it. No two entries of a row are equal modulo 64. Every listed block holds some token of the query block's rollout. `key_segments`: rollout numbers never fall along the context; all query tokens lie in the last rollout.
All inputs are finite; a program needn't handle non-finite values.
Results may differ from the reference program's by a relative error of at most 0.014.
Values may be sent and summed in bfloat16 or wider, within the bound.
A program may use at most 64 MiB of HBM per device.

```python
import jax
import jax.numpy as jnp
from jax import lax

H = 64
DC = 512
DR = 64
DN = 128
DV = 128
BLK = 128
TOPB = 16
KB_DEV = 16
DKV = 576
N_CTX = 64


def rollout_start(key):
    return jax.random.randint(key, (), 1, ((KB_DEV - 2) * N_CTX + 1) * BLK + 1)


def cache_base(key):
    normal = jnp.clip(jax.random.normal(key, (KB_DEV * N_CTX * BLK, DKV), jnp.float32), -6.0, 6.0)
    return normal


def draw_key_segments(key, part):
    start = rollout_start(key)
    key = jax.random.fold_in(key, 3)
    first = jax.random.randint(key, (), 0, start)
    position = jnp.arange(KB_DEV * N_CTX * BLK, dtype=jnp.int32).reshape(KB_DEV * N_CTX, BLK)
    return (position >= first).astype(jnp.int32) + (position >= start).astype(jnp.int32)


def draw_block_lists(key, part):
    start = rollout_start(key)
    key = jax.random.fold_in(key, 5)
    first_block = start // BLK

    def one_row(row_key, row):
        perm_key, level_key = jax.random.split(row_key)
        others = jax.random.permutation(perm_key, N_CTX - 1)[:TOPB - 1].astype(jnp.int32)
        residue = others + (others >= row).astype(jnp.int32)
        highest = jnp.where(residue < row, KB_DEV - 1, KB_DEV - 2).astype(jnp.int32)
        lowest = jnp.maximum(0, (first_block - residue + N_CTX - 1) // N_CTX).astype(jnp.int32)
        chosen = jax.random.randint(level_key, (TOPB - 1,), lowest, highest + 1)
        own_block = jnp.reshape((KB_DEV - 1) * N_CTX + row, (1,))
        return jnp.concatenate([own_block, chosen * N_CTX + residue]).astype(jnp.int32)
    row_keys = jax.random.split(key, N_CTX)
    return jax.vmap(one_row)(row_keys, jnp.arange(N_CTX, dtype=jnp.int32))


def draw_latent_cache(key, part):
    base = cache_base(key)
    return base.reshape(KB_DEV, N_CTX * BLK, DKV).astype(jnp.bfloat16)


def draw_queries(key, part):
    key = jax.random.fold_in(key, 9)
    values = jnp.clip(jax.random.normal(key, (N_CTX * BLK, H, DKV), jnp.float32), -6.0, 6.0)
    return values.astype(jnp.bfloat16)


def block_levels(own_key, shape, cuts, low, largest):
    gain = 1.0
    for axis_at, blocks in cuts:
        draws = jax.random.uniform(jax.random.fold_in(jax.random.fold_in(own_key, 6), axis_at), (blocks,), jnp.float32, low / len(cuts), largest / len(cuts))
        gain = gain * jnp.repeat(jnp.exp(draws), shape[axis_at] // blocks).reshape((-1,) + (1,) * (len(shape) - 1 - axis_at))
    return gain


def bell_draw(own_key, shape, deviation, bound, cuts=(), held_as=jnp.bfloat16):
    values = jax.random.normal(own_key, shape, jnp.float32) * deviation
    if len(cuts) > 0:
        values = block_levels(own_key, shape, cuts, -0.22, 0.18) * values
    return jnp.clip(values, min=-bound, max=bound).astype(held_as)


def setup_inputs(seed: int = 0) -> dict:
    arg_keys = jax.random.split(jax.random.key(seed), 6)
    return {
        "queries": draw_queries(jax.random.fold_in(arg_keys[5], 71), 0),
        "latent_cache": draw_latent_cache(jax.random.fold_in(arg_keys[5], 71), 0),
        "key_segments": draw_key_segments(jax.random.fold_in(arg_keys[5], 71), 0),
        "block_lists": draw_block_lists(jax.random.fold_in(arg_keys[5], 71), 0),
        "value_up": bell_draw(arg_keys[4], (H, DC, DV), (DC // 16) ** -0.5, 1.0, ((0, 8),)),
    }


def reference(queries, latent_cache, key_segments, block_lists, value_up):
    blocks = latent_cache.reshape(KB_DEV * N_CTX, BLK, DKV)
    grouped = queries.reshape(N_CTX, BLK, H, DKV)
    scale = (DN + DR) ** -0.5
    value_wide = value_up.astype(jnp.float32)
    token_index = jnp.arange(BLK, dtype=jnp.int32)

    def one_block(args):
        index, block_queries, listed = args
        key_rows = blocks[listed].reshape(TOPB * BLK, DKV).astype(jnp.float32)
        key_pos = (listed[:, None] * BLK + token_index[None, :]).reshape(-1)
        key_seg = key_segments[listed].reshape(-1)
        own_block = (KB_DEV - 1) * N_CTX + index
        query_pos = own_block * BLK + token_index
        query_seg = key_segments[own_block]
        allowed = (key_pos[None, :] <= query_pos[:, None]) & (key_seg[None, :] == query_seg[:, None])
        scores = jnp.einsum("qhd,kd->qhk", block_queries.astype(jnp.float32), key_rows) * scale
        row_max = jnp.max(jnp.where(allowed[:, None, :], scores, -jnp.inf), axis=2, keepdims=True)
        weights = jnp.where(allowed[:, None, :], jnp.exp(scores - row_max), 0.0)
        probs = (weights / jnp.sum(weights, axis=2, keepdims=True)).astype(jnp.bfloat16)
        latent_out = jnp.einsum("qhk,kc->qhc", probs.astype(jnp.float32), key_rows[:, :DC]).astype(jnp.bfloat16)
        values = jnp.einsum("qhc,hcv->qhv", latent_out.astype(jnp.float32), value_wide).astype(jnp.bfloat16)
        return values.reshape(BLK, H * DV)

    result = lax.map(one_block, (jnp.arange(N_CTX, dtype=jnp.int32), grouped, block_lists))
    return result.reshape(N_CTX * BLK, H * DV)
```

```python
import functools

import jax
import jax.numpy as jnp
from jax import lax
from jax.experimental import pallas as pl
from jax.experimental.pallas import tpu as pltpu
from jax.sharding import PartitionSpec as P

DC = 512
DR = 64
DN = 128
NEG = -1e30
EXP2_SCALE = (DN + DR) ** (-0.5) * 1.4426950408889634


def attention_kernel(q_ref, k_ref, vup_ref, bias_ref, o_ref, q32, qh, m_ref, l_ref, acc):
    heads = vup_ref.shape[0]
    tokens = q_ref.shape[0]
    chunks = k_ref.shape[0]
    rows = heads * tokens
    depth = q_ref.shape[2]
    for start in range(0, depth, 128):
        cols = min(128, depth - start)
        part = q_ref[:, :, start:start + cols].astype(jnp.float32).reshape(rows, cols)
        if cols < 128:
            part = jnp.concatenate([part, part], axis=1)
        q32[...] = part
        for h in range(heads):
            column = q32[pl.ds(h, tokens, stride=heads), :].astype(jnp.bfloat16)
            qh[h, :, start:start + cols] = column[:, :cols]
    m_ref[...] = jnp.full_like(m_ref, NEG)
    l_ref[...] = jnp.zeros_like(l_ref)
    acc[...] = jnp.zeros_like(acc)

    def one_chunk(c, carry):
        keys = k_ref[c]
        bias = bias_ref[c]
        for h in range(heads):
            s = lax.dot_general(
                qh[h], keys, (((1,), (1,)), ((), ())), preferred_element_type=jnp.float32
            )
            s = s + bias
            m_old = m_ref[h]
            m_new = jnp.maximum(m_old, jnp.max(s, axis=1, keepdims=True))
            alpha = jnp.exp2((m_old - m_new) * EXP2_SCALE)
            p = jnp.exp2((s - m_new[:, :1]) * EXP2_SCALE)
            half = p.shape[1] // 2
            l_ref[h] = l_ref[h] * alpha + (p[:, :half] + p[:, half:])
            m_ref[h] = m_new
            pv = jnp.dot(p.astype(jnp.bfloat16), keys[:, :DC], preferred_element_type=jnp.float32)
            acc[h] = acc[h] * alpha[:, :1] + pv
        return carry

    lax.fori_loop(0, chunks, one_chunk, 0)
    width = vup_ref.shape[2]
    for h in range(heads):
        total = jnp.sum(l_ref[h], axis=1, keepdims=True)
        latent = (acc[h] / total).astype(jnp.bfloat16)
        o_ref[:, h * width:(h + 1) * width] = jnp.dot(
            latent, vup_ref[h], preferred_element_type=jnp.float32
        ).astype(o_ref.dtype)


def attention(queries, keys, value_up, bias):
    tokens, heads, depth = queries.shape
    rows = tokens * heads
    vmem = pl.BlockSpec(memory_space=pltpu.VMEM)
    return pl.pallas_call(
        attention_kernel,
        out_shape=jax.ShapeDtypeStruct((tokens, heads * value_up.shape[2]), jnp.bfloat16),
        in_specs=[vmem] * 4,
        out_specs=vmem,
        scratch_shapes=[
            pltpu.VMEM((rows, 128), jnp.float32),
            pltpu.VMEM((heads, tokens, depth), jnp.bfloat16),
            pltpu.VMEM((heads, tokens, 128), jnp.float32),
            pltpu.VMEM((heads, tokens, 128), jnp.float32),
            pltpu.VMEM((heads, tokens, DC), jnp.float32),
        ],
        compiler_params=pltpu.CompilerParams(vmem_limit_bytes=40 * 1024 * 1024),
    )(queries, keys, value_up, bias)


def shards(queries, latent_cache, key_segments, block_lists, value_up):
    owners = lax.axis_size("ctx")
    own_index = lax.axis_index("ctx")
    depth, piece, width = latent_cache.shape
    pieces = lax.axis_size("tp")
    requests = lax.all_gather(block_lists, "ctx", axis=0, tiled=True)
    matched = requests % owners == own_index
    level = jnp.sum(jnp.where(matched, requests // owners, 0), axis=1)
    outgoing = latent_cache[level]
    incoming = lax.all_to_all(outgoing, "ctx", split_axis=0, concat_axis=0, tiled=True)
    wanted = block_lists[0]
    picked = incoming[wanted % owners]
    gathered = lax.all_gather(picked, "tp", axis=0)
    keys = gathered.reshape(pieces, -1, width)
    own_block = (depth - 1) * owners + own_index
    block_len = key_segments.shape[1]
    token = jnp.arange(block_len, dtype=jnp.int32)
    pos = wanted[:, None] * block_len + token[None, :]
    query_seg = key_segments[own_block, block_len - 1]
    in_rollout = key_segments[wanted] == query_seg
    allowed = in_rollout[None] & (pos[None] <= (own_block * block_len + token)[:, None, None])
    bias = jnp.where(allowed, 0.0, NEG).astype(jnp.float32)
    bias = bias.reshape(block_len, -1, pieces, piece).transpose(2, 0, 1, 3)
    bias = bias.reshape(pieces, block_len, -1)
    return attention(queries, keys, value_up, bias)


def solution(mesh):
    return jax.shard_map(
        shards,
        mesh=mesh,
        in_specs=(
            P("ctx", "tp", None),
            P(None, ("ctx", "tp"), None),
            P(),
            P("ctx", None),
            P("tp", None, None),
        ),
        out_specs=P("ctx", "tp"),
        check_vma=False,
    )
```

```python
import jax
import jax.numpy as jnp
from jax import lax
from jax.experimental import pallas as pl
from jax.experimental.pallas import tpu as pltpu
from jax.sharding import PartitionSpec as P

MESH = pl.DeviceIdType.MESH
DC = 512
DR = 64
DN = 128
BIG = 1e30
EXP2_SCALE = (DN + DR) ** (-0.5) * 1.4426950408889634
NZ, NX = 4, 8
CHIPS = NZ * NX
RING = 8
HEADS = 8
TOKENS = 128
PIECE = 16
LISTED = 16
LEVELS = 16
ROWS = HEADS * TOKENS
KEYS = LISTED * PIECE
LANES = 128
PARTS = 2
MESSAGE = (4, 5)
CHUNK = (32, 40)


def body(
    lists, cache, q_hbm, vup_hbm, seg_hbm, out,
    q_in, vup, seg, both, want_in, comb, levels,
    send_a, send_b, recv_a, recv_b, gat_a, gat_b,
    qa, kcat, valid, m_ref, l_ref, acc,
    local_sem, level_sem, sib_send, sib_recv, want_send, want_recv,
    mess_send, mess_recv, ring_send, ring_recv,
):
    me = lax.axis_index("ctx")
    t = lax.axis_index("tp")
    chip = me // 2
    core = me % 2
    z = chip // NX
    x = chip % NX
    right = (t + 1) % RING
    left = (t + RING - 1) % RING
    sends, recvs, gats = (send_a, send_b), (recv_a, recv_b), (gat_a, gat_b)

    def other(o):
        return ((z + o // NX) % NZ) * NX + (x + o % NX) % NX

    barrier = pltpu.get_barrier_semaphore()

    def greet(o, carry):
        pl.semaphore_signal(
            barrier, inc=1, device_id=(other(o) * 2 + core, t), device_id_type=MESH
        )
        return carry

    lax.fori_loop(1, CHIPS, greet, 0)
    for peer in ((chip * 2 + 1 - core, t), (me, right), (me, left)):
        pl.semaphore_signal(barrier, inc=1, device_id=peer, device_id_type=MESH)

    locals_ = [
        pltpu.make_async_copy(q_hbm, q_in, local_sem.at[0]),
        pltpu.make_async_copy(vup_hbm, vup, local_sem.at[1]),
        pltpu.make_async_copy(seg_hbm, seg, local_sem.at[2]),
    ]
    for copy in locals_:
        copy.start()

    lane8 = lax.broadcasted_iota(jnp.int32, (8, LANES), 1)
    row = jnp.zeros((8, LANES), jnp.int32)
    for j in range(LISTED):
        entry = lists[0, j]
        row = jnp.where(lane8 == (entry & 63), entry >> 6, row)
    want_in[chip] = row

    for level in range(LEVELS):
        for i in range(4):
            both[core, level, i] = cache[level, :, i * LANES:(i + 1) * LANES]
        rope = cache[level, :, DC:DC + DR]
        both[core, level, 4] = jnp.concatenate([rope, rope], axis=1)

    pl.semaphore_wait(barrier, CHIPS - 1 + 3)

    def want_copy(o):
        return pltpu.make_async_remote_copy(
            src_ref=want_in.at[chip], dst_ref=want_in.at[chip],
            send_sem=want_send.at[o], recv_sem=want_recv.at[chip],
            device_id=(other(o) * 2 + core, t), device_id_type=MESH,
        )

    def want_start(o, carry):
        want_copy(o).start()
        return carry

    lax.fori_loop(1, CHIPS, want_start, 0)
    sibling = pltpu.make_async_remote_copy(
        src_ref=both.at[core], dst_ref=both.at[core],
        send_sem=sib_send, recv_sem=sib_recv,
        device_id=(chip * 2 + 1 - core, t), device_id_type=MESH,
    )
    sibling.start()

    def want_wait(o, carry):
        source = other(o)
        pltpu.make_async_remote_copy(
            src_ref=want_in.at[source], dst_ref=want_in.at[source],
            send_sem=want_send.at[o], recv_sem=want_recv.at[source],
            device_id=(source * 2 + core, t), device_id_type=MESH,
        ).wait_recv()
        return carry

    lax.fori_loop(1, CHIPS, want_wait, 0)
    for s in range(CHIPS):
        comb[s:s + 1, :] = want_in[s, 0:1, :]
    to_scalar = pltpu.make_async_copy(comb, levels, level_sem)
    to_scalar.start()
    pltpu.make_async_remote_copy(
        src_ref=both.at[1 - core], dst_ref=both.at[1 - core],
        send_sem=sib_send, recv_sem=sib_recv,
        device_id=(chip * 2 + 1 - core, t), device_id_type=MESH,
    ).wait_recv()
    to_scalar.wait()

    lane16 = lax.broadcasted_iota(jnp.int32, (PIECE, LANES), 1)

    def fill(part, dest, ref, slot):
        at0 = levels[dest, 2 * chip]
        at1 = levels[dest, 2 * chip + 1]
        for i in range(2):
            ref[slot, i] = both[0, at0, 2 * part + i]
            ref[slot, 2 + i] = both[1, at1, 2 * part + i]
        if part == 1:
            ref[slot, 4] = jnp.where(lane16 < DR, both[0, at0, 4], both[1, at1, 4])

    def message(part, o):
        dest = other(o)
        return pltpu.make_async_remote_copy(
            src_ref=sends[part].at[o], dst_ref=recvs[part].at[chip],
            send_sem=mess_send.at[part, o], recv_sem=mess_recv.at[part, chip],
            device_id=(dest * 2 + core, t), device_id_type=MESH,
        )

    for part in range(PARTS):
        def send_one(o, carry, part=part):
            fill(part, other(o), sends[part], o)
            message(part, o).start()
            return carry

        lax.fori_loop(1, CHIPS, send_one, 0)
        fill(part, chip, recvs[part], chip)

    locals_[0].wait()
    for h in range(HEADS):
        rows = slice(h * TOKENS, (h + 1) * TOKENS)
        for i in range(4):
            qa[rows, i * LANES:(i + 1) * LANES] = q_in[h, i * LANES:(i + 1) * LANES, :].T
        rope = q_in[h, DC:DC + DR, :]
        qa[rows, DC:] = jnp.concatenate([rope, rope], axis=0).T

    locals_[2].wait()
    last = seg[pl.ds((LEVELS - 1) * CHIPS * 2 + me, 1), :]
    query_seg = last[:, LANES - 1:LANES]
    for j in range(LISTED):
        place = (j % 2) * (LISTED // 2) + j // 2
        rollout = seg[pl.ds(lists[0, j], 1), :]
        valid[place:place + 1, :] = jnp.where(rollout == query_seg, 1.0, 0.0)

    m_ref[...] = jnp.full_like(m_ref, -BIG)
    l_ref[...] = jnp.zeros_like(l_ref)
    acc[...] = jnp.zeros_like(acc)

    def wait_messages(part):
        def one(o, carry):
            source = other(o)
            pltpu.make_async_remote_copy(
                src_ref=sends[part].at[o], dst_ref=recvs[part].at[source],
                send_sem=mess_send.at[part, o], recv_sem=mess_recv.at[part, source],
                device_id=(source * 2 + core, t), device_id_type=MESH,
            ).wait_recv()
            return carry

        lax.fori_loop(1, CHIPS, one, 0)

    def pick(part):
        halves = []
        for j in range(LISTED):
            place = (j % 2) * (LISTED // 2) + j // 2
            residue = lists[0, j] & 63
            source = residue >> 1
            parity = residue & 1
            for i in range(2):
                gats[part][t, i * LISTED + place] = recvs[part][source, parity * 2 + i]
            if part == 1:
                tile = recvs[part][source, 4]
                low, high = tile[:, :DR], tile[:, DR:]
                halves.append(jnp.where(parity == 0, low, high))
                if j % 2 == 1:
                    gats[part][t, 2 * LISTED + j // 2] = jnp.concatenate(halves, axis=1)
                    halves = []

    def ring(part, direction, step, half):
        whole = CHUNK[part]
        origin = (t - step + 1 + RING) % RING if direction == 0 else (t + step - 1) % RING
        start, count = (0, whole) if not half else (direction * (whole // 2), whole // 2)
        piece = gats[part].at[origin, pl.ds(start, count)]
        return pltpu.make_async_remote_copy(
            src_ref=piece, dst_ref=piece,
            send_sem=ring_send.at[part, direction, step],
            recv_sem=ring_recv.at[part, direction, step],
            device_id=(me, right if direction == 0 else left), device_id_type=MESH,
        )

    def ring_wait(part, direction, step, half):
        whole = CHUNK[part]
        origin = (t - step + RING) % RING if direction == 0 else (t + step) % RING
        start, count = (0, whole) if not half else (direction * (whole // 2), whole // 2)
        piece = gats[part].at[origin, pl.ds(start, count)]
        pltpu.make_async_remote_copy(
            src_ref=piece, dst_ref=piece,
            send_sem=ring_send.at[part, direction, step],
            recv_sem=ring_recv.at[part, direction, step],
            device_id=(me, right if direction == 0 else left), device_id_type=MESH,
        ).wait_recv()

    def ring_advance(part, step):
        for direction in range(2):
            ring_wait(part, direction, step, False)

            @pl.when(step < 3)
            def _(direction=direction):
                ring(part, direction, step + 1, False).start()

            @pl.when(step == 3)
            def _(direction=direction):
                ring(part, direction, 4, True).start()

    wait_messages(0)
    pick(0)
    for direction in range(2):
        ring(0, direction, 1, False).start()

    def first_part(step, carry):
        ring_advance(0, step)
        return carry

    lax.fori_loop(1, 4, first_part, 0)
    wait_messages(1)
    pick(1)
    for direction in range(2):
        ring(1, direction, 1, False).start()
    for direction in range(2):
        ring_wait(0, direction, 4, True)

    lane_r = lax.broadcasted_iota(jnp.int32, (LISTED // 2 * PIECE, LANES), 1)

    def attend(origin):
        for i in range(2):
            for part in range(2):
                at = (2 * part + i) * LANES
                kcat[:, at:at + LANES] = gats[part][
                    origin, i * LISTED:(i + 1) * LISTED
                ].reshape(KEYS, LANES)
        rope = gat_b[origin, 2 * LISTED:].reshape(KEYS // 2, LANES)
        kcat[:KEYS // 2, DC:] = jnp.where(lane_r < DR, rope, jnp.zeros_like(rope))
        kcat[KEYS // 2:, DC:] = jnp.where(lane_r < DR, jnp.zeros_like(rope), rope)
        token = lax.broadcasted_iota(jnp.int32, (LANES, KEYS), 0)
        key = lax.broadcasted_iota(jnp.int32, (LANES, KEYS), 1)
        spread = jnp.where(token == origin * PIECE + key % PIECE, 1.0, 0.0).astype(jnp.bfloat16)
        seen = jnp.dot(valid[...].astype(jnp.bfloat16), spread, preferred_element_type=jnp.float32)
        place = lax.broadcasted_iota(jnp.int32, (LISTED, KEYS), 0)
        lane = lax.broadcasted_iota(jnp.int32, (LISTED, KEYS), 1)
        seen = jnp.sum(jnp.where(lane // PIECE == place, seen, 0.0), axis=0, keepdims=True)
        bias = jnp.broadcast_to((seen - 1.0) * BIG, (TOKENS, KEYS))
        query = lax.broadcasted_iota(jnp.int32, (TOKENS, KEYS), 0)
        column = lax.broadcasted_iota(jnp.int32, (TOKENS, KEYS), 1)
        later = (column < PIECE) & (origin * PIECE + column > query)
        bias = jnp.where(later, -BIG, bias)
        group = 4
        for g in range(HEADS // group):
            rows = pl.ds(g * group * TOKENS, group * TOKENS)
            s = lax.dot_general(
                qa[rows, :], kcat[...], (((1,), (1,)), ((), ())),
                preferred_element_type=jnp.float32,
            )
            s = (s.reshape(group, TOKENS, KEYS) + bias[None]).reshape(group * TOKENS, KEYS)
            m_old = m_ref[rows, :]
            m_new = jnp.maximum(m_old, jnp.max(s, axis=1, keepdims=True))
            alpha = jnp.exp2((m_old - m_new) * EXP2_SCALE)
            p = jnp.exp2((s - m_new[:, :1]) * EXP2_SCALE)
            l_ref[rows, :] = l_ref[rows, :] * alpha + (p[:, :LANES] + p[:, LANES:])
            m_ref[rows, :] = m_new
            pv = jnp.dot(
                p.astype(jnp.bfloat16), kcat[:, :DC], preferred_element_type=jnp.float32
            )
            acc[rows, :] = acc[rows, :] * alpha[:, :1] + pv

    def visit(n, carry):
        step = (n + 1) // 2

        @pl.when((n % 2 == 1) & (n < 7))
        def _():
            ring_advance(1, step)

        @pl.when(n == 7)
        def _():
            for direction in range(2):
                ring_wait(1, direction, 4, True)

        attend((t + RING + (1 - 2 * (n % 2)) * step) % RING)
        return carry

    lax.fori_loop(0, RING, visit, 0)

    locals_[1].wait()
    width = vup.shape[2]
    for h in range(HEADS):
        rows = pl.ds(h * TOKENS, TOKENS)
        total = jnp.sum(l_ref[rows, :], axis=1, keepdims=True)
        latent = (acc[rows, :] / total).astype(jnp.bfloat16)
        out[:, h * width:(h + 1) * width] = jnp.dot(
            latent, vup[h], preferred_element_type=jnp.float32
        ).astype(out.dtype)

    sibling.wait_send()

    def sent(o, carry):
        want_copy(o).wait_send()
        for part in range(PARTS):
            message(part, o).wait_send()
        return carry

    lax.fori_loop(1, CHIPS, sent, 0)
    for part in range(PARTS):
        for direction in range(2):
            for step in range(1, 5):
                ring(part, direction, step, step == 4).wait_send()


def shards(queries, latent_cache, key_segments, block_lists, value_up):
    tokens, heads, width = queries.shape
    bf16, f32 = jnp.bfloat16, jnp.float32
    tile = (PIECE, LANES)
    vmem = pl.BlockSpec(memory_space=pltpu.VMEM)
    anywhere = pl.BlockSpec(memory_space=pl.ANY)
    return pl.pallas_call(
        body,
        out_shape=jax.ShapeDtypeStruct((tokens, heads * value_up.shape[2]), bf16),
        in_specs=[pl.BlockSpec(memory_space=pltpu.SMEM), vmem, anywhere, anywhere, anywhere],
        out_specs=vmem,
        scratch_shapes=[
            pltpu.VMEM((heads, width, tokens), bf16),
            pltpu.VMEM(value_up.shape, bf16),
            pltpu.VMEM(key_segments.shape, jnp.int32),
            pltpu.VMEM((2, LEVELS, 5) + tile, bf16),
            pltpu.VMEM((CHIPS, 8, LANES), jnp.int32),
            pltpu.VMEM((CHIPS, LANES), jnp.int32),
            pltpu.SMEM((CHIPS, LANES), jnp.int32),
            pltpu.VMEM((CHIPS, MESSAGE[0]) + tile, bf16),
            pltpu.VMEM((CHIPS, MESSAGE[1]) + tile, bf16),
            pltpu.VMEM((CHIPS, MESSAGE[0]) + tile, bf16),
            pltpu.VMEM((CHIPS, MESSAGE[1]) + tile, bf16),
            pltpu.VMEM((RING, CHUNK[0]) + tile, bf16),
            pltpu.VMEM((RING, CHUNK[1]) + tile, bf16),
            pltpu.VMEM((ROWS, DC + LANES), bf16),
            pltpu.VMEM((KEYS, DC + LANES), bf16),
            pltpu.VMEM((LISTED, LANES), f32),
            pltpu.VMEM((ROWS, LANES), f32),
            pltpu.VMEM((ROWS, LANES), f32),
            pltpu.VMEM((ROWS, DC), f32),
            pltpu.SemaphoreType.DMA((3,)),
            pltpu.SemaphoreType.DMA,
            pltpu.SemaphoreType.DMA,
            pltpu.SemaphoreType.DMA,
            pltpu.SemaphoreType.DMA((CHIPS,)),
            pltpu.SemaphoreType.DMA((CHIPS,)),
            pltpu.SemaphoreType.DMA((PARTS, CHIPS)),
            pltpu.SemaphoreType.DMA((PARTS, CHIPS)),
            pltpu.SemaphoreType.DMA((PARTS, 2, 5)),
            pltpu.SemaphoreType.DMA((PARTS, 2, 5)),
        ],
        compiler_params=pltpu.CompilerParams(
            collective_id=0, has_side_effects=True, vmem_limit_bytes=60 * 1024 * 1024
        ),
    )(block_lists, latent_cache, queries.transpose(1, 2, 0), value_up, key_segments)


def solution(mesh):
    return jax.shard_map(
        shards,
        mesh=mesh,
        in_specs=(
            P("ctx", "tp", None),
            P(None, ("ctx", "tp"), None),
            P(),
            P("ctx", None),
            P("tp", None, None),
        ),
        out_specs=P("ctx", "tp"),
        check_vma=False,
    )
```

```python
import jax
import jax.numpy as jnp
from jax import lax
from jax.experimental import pallas as pl
from jax.experimental.pallas import tpu as pltpu
from jax.sharding import PartitionSpec as P

MESH = pl.DeviceIdType.MESH
DC = 512
DR = 64
DN = 128
BIG = 1e30
EXP2_SCALE = (DN + DR) ** (-0.5) * 1.4426950408889634
NZ, NX = 4, 8
GROUP = 2 * NX
RING = 8
HEADS = 8
TOKENS = 128
PIECE = 16
LISTED = 16
LEVELS = 16
ROWS = HEADS * TOKENS
KEYS = LISTED * PIECE
LANES = 128
PARTS = 4
ROPE = 1
BATCH = 4
SHARD = tuple(24 if part == ROPE else 16 for part in range(PARTS))
MESSAGE = tuple(6 if part == ROPE else 4 for part in range(PARTS))
CHUNK = SHARD


def body(
    lists, cache, q_hbm, vup_hbm, seg_hbm, out, *scratch
):
    planes, sends, recvs, gats = (scratch[PARTS * i:PARTS * (i + 1)] for i in range(4))
    (
        q_in, vup, seg, want_in, comb, levels,
        qa, kcat, valid, m_ref, l_ref, acc,
        local_sem, level_sem, want_send, want_recv, plane_send, plane_recv,
        mess_send, mess_recv, ring_send, ring_recv,
    ) = scratch[4 * PARTS:]
    me = lax.axis_index("ctx")
    t = lax.axis_index("tp")
    z = me // GROUP
    spot = me % GROUP
    x = spot // 2
    core = spot % 2
    right = (t + 1) % RING
    left = (t + RING - 1) % RING
    above = ((z + 1) % NZ) * GROUP + spot
    below = ((z + NZ - 1) % NZ) * GROUP + spot

    def other(o):
        return ((x + o // 2) % NX) * 2 + (core + o % 2) % 2

    barrier = pltpu.get_barrier_semaphore()
    for peer in ((above, t), (below, t), (me, right), (me, left)):
        pl.semaphore_signal(barrier, inc=1, device_id=peer, device_id_type=MESH)

    def greet(o, carry):
        pl.semaphore_signal(
            barrier, inc=1, device_id=(z * GROUP + other(o), t), device_id_type=MESH
        )
        return carry

    lax.fori_loop(1, GROUP, greet, 0)

    locals_ = [
        pltpu.make_async_copy(q_hbm, q_in, local_sem.at[0]),
        pltpu.make_async_copy(vup_hbm, vup, local_sem.at[1]),
        pltpu.make_async_copy(seg_hbm, seg, local_sem.at[2]),
    ]
    for copy in locals_:
        copy.start()

    lane8 = lax.broadcasted_iota(jnp.int32, (8, LANES), 1)
    row = jnp.zeros((8, LANES), jnp.int32)
    for j in range(LISTED):
        entry = lists[0, j]
        row = jnp.where(lane8 == (entry & 63), entry >> 6, row)
    want_in[spot] = row

    for level in range(LEVELS):
        for part in range(PARTS):
            planes[part][z, level] = cache[level, :, part * LANES:(part + 1) * LANES]
        if level % 2 == 1:
            planes[ROPE][z, LEVELS + level // 2] = jnp.concatenate(
                [cache[level - 1, :, DC:], cache[level, :, DC:]], axis=1
            )

    def plane_copy(part, direction, step, arriving):
        whole = SHARD[part]
        hops = step if arriving else step - 1
        origin = (z + NZ - hops) % NZ if direction == 0 else (z + hops) % NZ
        start, count = (0, whole) if step == 1 else (direction * (whole // 2), whole // 2)
        piece = planes[part].at[origin, pl.ds(start, count)]
        return pltpu.make_async_remote_copy(
            src_ref=piece, dst_ref=piece,
            send_sem=plane_send.at[part, direction, step],
            recv_sem=plane_recv.at[part, direction, step],
            device_id=(above if direction == 0 else below, t), device_id_type=MESH,
        )

    pl.semaphore_wait(barrier, GROUP - 1 + 4)

    def want_copy(o):
        return pltpu.make_async_remote_copy(
            src_ref=want_in.at[spot], dst_ref=want_in.at[spot],
            send_sem=want_send.at[o], recv_sem=want_recv.at[spot],
            device_id=(z * GROUP + other(o), t), device_id_type=MESH,
        )

    def want_start(o, carry):
        want_copy(o).start()
        return carry

    def plane_open(part):
        for direction in range(2):
            plane_copy(part, direction, 1, False).start()

    plane_open(0)
    lax.fori_loop(1, GROUP, want_start, 0)
    plane_open(1)

    locals_[0].wait()
    for h in range(HEADS):
        rows = slice(h * TOKENS, (h + 1) * TOKENS)
        for i in range(4):
            qa[rows, i * LANES:(i + 1) * LANES] = q_in[h, i * LANES:(i + 1) * LANES, :].T
        rope = q_in[h, DC:DC + DR, :]
        qa[rows, DC:] = jnp.concatenate([rope, rope], axis=0).T

    def plane_pass(part):
        for direction in range(2):
            plane_copy(part, direction, 1, True).wait_recv()
            plane_copy(part, direction, 2, False).start()

    plane_pass(0)
    plane_open(2)

    def want_wait(o, carry):
        source = other(o)
        pltpu.make_async_remote_copy(
            src_ref=want_in.at[source], dst_ref=want_in.at[source],
            send_sem=want_send.at[o], recv_sem=want_recv.at[source],
            device_id=(z * GROUP + source, t), device_id_type=MESH,
        ).wait_recv()
        return carry

    lax.fori_loop(1, GROUP, want_wait, 0)
    for s in range(GROUP):
        comb[s:s + 1, :] = want_in[s, 0:1, :]
    to_scalar = pltpu.make_async_copy(comb, levels, level_sem)
    to_scalar.start()
    to_scalar.wait()

    def fill(part, dest, ref, slot):
        halves = []
        for plane in range(NZ):
            level = levels[dest, plane * GROUP + spot]
            ref[slot, plane] = planes[part][plane, level]
            if part == ROPE:
                tile = planes[part][plane, LEVELS + (level >> 1)]
                halves.append(jnp.where((level & 1) == 0, tile[:, :DR], tile[:, DR:]))
                if plane % 2 == 1:
                    ref[slot, NZ + plane // 2] = jnp.concatenate(halves, axis=1)
                    halves = []

    def message(part, o):
        return pltpu.make_async_remote_copy(
            src_ref=sends[part].at[o], dst_ref=recvs[part].at[spot],
            send_sem=mess_send.at[part, o], recv_sem=mess_recv.at[part, spot],
            device_id=(z * GROUP + other(o), t), device_id_type=MESH,
        )

    def plane_close(part):
        for direction in range(2):
            plane_copy(part, direction, 2, True).wait_recv()

        def send_one(o, carry):
            fill(part, other(o), sends[part], o)
            message(part, o).start()
            return carry

        lax.fori_loop(1, GROUP, send_one, 0)
        fill(part, spot, recvs[part], spot)

    locals_[2].wait()
    last = seg[pl.ds((LEVELS - 1) * NZ * GROUP + me, 1), :]
    query_seg = last[:, LANES - 1:LANES]
    for j in range(LISTED):
        place = (j % 2) * (LISTED // 2) + j // 2
        rollout = seg[pl.ds(lists[0, j], 1), :]
        valid[place:place + 1, :] = jnp.where(rollout == query_seg, 1.0, 0.0)

    m_ref[...] = jnp.full_like(m_ref, -BIG)
    l_ref[...] = jnp.zeros_like(l_ref)
    acc[...] = jnp.zeros_like(acc)

    def wait_messages(part):
        def one(o, carry):
            source = other(o)
            pltpu.make_async_remote_copy(
                src_ref=sends[part].at[o], dst_ref=recvs[part].at[source],
                send_sem=mess_send.at[part, o], recv_sem=mess_recv.at[part, source],
                device_id=(z * GROUP + source, t), device_id_type=MESH,
            ).wait_recv()
            return carry

        lax.fori_loop(1, GROUP, one, 0)

    def pick(part):
        halves = []
        for j in range(LISTED):
            place = (j % 2) * (LISTED // 2) + j // 2
            residue = lists[0, j] & 63
            plane = residue >> 4
            source = residue & 15
            gats[part][t, place] = recvs[part][source, plane]
            if part == ROPE:
                tile = recvs[part][source, NZ + (plane >> 1)]
                halves.append(jnp.where((plane & 1) == 0, tile[:, :DR], tile[:, DR:]))
                if j % 2 == 1:
                    gats[part][t, LISTED + j // 2] = jnp.concatenate(halves, axis=1)
                    halves = []

    def ring(part, direction, step, arriving):
        whole = CHUNK[part]
        hops = step if arriving else step - 1
        origin = (t + RING - hops) % RING if direction == 0 else (t + hops) % RING
        start, count = (0, whole) if step < 4 else (direction * (whole // 2), whole // 2)
        piece = gats[part].at[origin, pl.ds(start, count)]
        return pltpu.make_async_remote_copy(
            src_ref=piece, dst_ref=piece,
            send_sem=ring_send.at[part, direction, step],
            recv_sem=ring_recv.at[part, direction, step],
            device_id=(me, right if direction == 0 else left), device_id_type=MESH,
        )

    def ring_open(part):
        wait_messages(part)
        pick(part)
        for direction in range(2):
            ring(part, direction, 1, False).start()

    def ring_pass(part, step):
        for direction in range(2):
            ring(part, direction, step, True).wait_recv()
            if step < 4:
                ring(part, direction, step + 1, False).start()

    lane_r = lax.broadcasted_iota(jnp.int32, (KEYS // 2, LANES), 1)

    def attend(origins):
        count = len(origins) * KEYS
        biases = []
        for n, origin in enumerate(origins):
            first = slice(n * KEYS, n * KEYS + KEYS // 2)
            second = slice(n * KEYS + KEYS // 2, (n + 1) * KEYS)
            for part in range(PARTS):
                kcat[n * KEYS:(n + 1) * KEYS, part * LANES:(part + 1) * LANES] = gats[part][
                    origin, :LISTED
                ].reshape(KEYS, LANES)
            rope = gats[ROPE][origin, LISTED:].reshape(KEYS // 2, LANES)
            kcat[first, DC:] = jnp.where(lane_r < DR, rope, jnp.zeros_like(rope))
            kcat[second, DC:] = jnp.where(lane_r < DR, jnp.zeros_like(rope), rope)
            token = lax.broadcasted_iota(jnp.int32, (LANES, KEYS), 0)
            key = lax.broadcasted_iota(jnp.int32, (LANES, KEYS), 1)
            spread = jnp.where(token == origin * PIECE + key % PIECE, 1.0, 0.0).astype(jnp.bfloat16)
            seen = jnp.dot(
                valid[...].astype(jnp.bfloat16), spread, preferred_element_type=jnp.float32
            )
            place = lax.broadcasted_iota(jnp.int32, (LISTED, KEYS), 0)
            lane = lax.broadcasted_iota(jnp.int32, (LISTED, KEYS), 1)
            seen = jnp.sum(jnp.where(lane // PIECE == place, seen, 0.0), axis=0, keepdims=True)
            bias = jnp.broadcast_to((seen - 1.0) * BIG, (TOKENS, KEYS))
            query = lax.broadcasted_iota(jnp.int32, (TOKENS, KEYS), 0)
            column = lax.broadcasted_iota(jnp.int32, (TOKENS, KEYS), 1)
            later = (column < PIECE) & (origin * PIECE + column > query)
            biases.append(jnp.where(later, -BIG, bias))
        bias = jnp.concatenate(biases, axis=1) if len(origins) > 1 else biases[0]
        for g in range(HEADS // BATCH):
            rows = pl.ds(g * BATCH * TOKENS, BATCH * TOKENS)
            s = lax.dot_general(
                qa[rows, :], kcat[:count, :], (((1,), (1,)), ((), ())),
                preferred_element_type=jnp.float32,
            )
            s = (s.reshape(BATCH, TOKENS, count) + bias[None]).reshape(BATCH * TOKENS, count)
            m_old = m_ref[rows, :]
            m_new = jnp.maximum(m_old, jnp.max(s, axis=1, keepdims=True))
            alpha = jnp.exp2((m_old - m_new) * EXP2_SCALE)
            p = jnp.exp2((s - m_new[:, :1]) * EXP2_SCALE)
            l_new = l_ref[rows, :] * alpha
            for at in range(0, count, LANES):
                l_new = l_new + p[:, at:at + LANES]
            l_ref[rows, :] = l_new
            m_ref[rows, :] = m_new
            pv = jnp.dot(
                p.astype(jnp.bfloat16), kcat[:count, :DC], preferred_element_type=jnp.float32
            )
            acc[rows, :] = acc[rows, :] * alpha[:, :1] + pv

    for act, part, step in (
        (plane_close, 0, 0), (plane_pass, 1, 0), (plane_open, 3, 0), (plane_pass, 2, 0),
        (plane_close, 1, 0), (ring_open, 0, 0), (plane_pass, 3, 0), (plane_close, 2, 0),
        (ring_pass, 0, 1), (plane_close, 3, 0), (ring_open, 1, 0), (ring_pass, 0, 2),
        (ring_open, 2, 0), (ring_pass, 0, 3), (ring_pass, 1, 1), (ring_open, 3, 0),
        (ring_pass, 2, 1), (ring_pass, 1, 2), (ring_pass, 3, 1),
    ):
        act(part, step) if act is ring_pass else act(part)
    attend([t])
    for part, step in ((0, 4), (2, 2), (1, 3), (3, 2)):
        ring_pass(part, step)
    attend([left, right])
    for part, step in ((2, 3), (3, 3)):
        ring_pass(part, step)
    attend([(t + 6) % RING, (t + 2) % RING])
    for part, step in ((1, 4), (2, 4), (3, 4)):
        ring_pass(part, step)
    attend([(t + 5) % RING, (t + 3) % RING])
    attend([(t + 4) % RING])

    locals_[1].wait()
    width = vup.shape[2]
    for h in range(HEADS):
        rows = pl.ds(h * TOKENS, TOKENS)
        total = jnp.sum(l_ref[rows, :], axis=1, keepdims=True)
        latent = (acc[rows, :] / total).astype(jnp.bfloat16)
        out[:, h * width:(h + 1) * width] = jnp.dot(
            latent, vup[h], preferred_element_type=jnp.float32
        ).astype(out.dtype)

    def sent(o, carry):
        want_copy(o).wait_send()
        for part in range(PARTS):
            message(part, o).wait_send()
        return carry

    lax.fori_loop(1, GROUP, sent, 0)
    for part in range(PARTS):
        for direction in range(2):
            for step in range(1, 3):
                plane_copy(part, direction, step, False).wait_send()
            for step in range(1, 5):
                ring(part, direction, step, False).wait_send()


def shards(queries, latent_cache, key_segments, block_lists, value_up):
    tokens, heads, width = queries.shape
    bf16, f32 = jnp.bfloat16, jnp.float32
    vmem = pl.BlockSpec(memory_space=pltpu.VMEM)
    anywhere = pl.BlockSpec(memory_space=pl.ANY)

    def tiles(outer, counts):
        return [pltpu.VMEM((outer, count, PIECE, LANES), bf16) for count in counts]

    sem = pltpu.SemaphoreType.DMA
    return pl.pallas_call(
        body,
        out_shape=jax.ShapeDtypeStruct((tokens, heads * value_up.shape[2]), bf16),
        in_specs=[pl.BlockSpec(memory_space=pltpu.SMEM), vmem, anywhere, anywhere, anywhere],
        out_specs=vmem,
        scratch_shapes=[
            *tiles(NZ, SHARD),
            *tiles(GROUP, MESSAGE),
            *tiles(GROUP, MESSAGE),
            *tiles(RING, CHUNK),
            pltpu.VMEM((heads, width, tokens), bf16),
            pltpu.VMEM(value_up.shape, bf16),
            pltpu.VMEM(key_segments.shape, jnp.int32),
            pltpu.VMEM((GROUP, 8, LANES), jnp.int32),
            pltpu.VMEM((GROUP, LANES), jnp.int32),
            pltpu.SMEM((GROUP, LANES), jnp.int32),
            pltpu.VMEM((ROWS, DC + LANES), bf16),
            pltpu.VMEM((2 * KEYS, DC + LANES), bf16),
            pltpu.VMEM((LISTED, LANES), f32),
            pltpu.VMEM((ROWS, LANES), f32),
            pltpu.VMEM((ROWS, LANES), f32),
            pltpu.VMEM((ROWS, DC), f32),
            sem((3,)),
            sem,
            sem((GROUP,)),
            sem((GROUP,)),
            sem((PARTS, 2, 3)),
            sem((PARTS, 2, 3)),
            sem((PARTS, GROUP)),
            sem((PARTS, GROUP)),
            sem((PARTS, 2, 5)),
            sem((PARTS, 2, 5)),
        ],
        compiler_params=pltpu.CompilerParams(
            collective_id=0, has_side_effects=True, vmem_limit_bytes=60 * 1024 * 1024
        ),
    )(block_lists, latent_cache, queries.transpose(1, 2, 0), value_up, key_segments)


def solution(mesh):
    return jax.shard_map(
        shards,
        mesh=mesh,
        in_specs=(
            P("ctx", "tp", None),
            P(None, ("ctx", "tp"), None),
            P(),
            P("ctx", None),
            P("tp", None, None),
        ),
        out_specs=P("ctx", "tp"),
        check_vma=False,
    )
```

```python
import jax
import jax.numpy as jnp
from jax import lax
from jax.experimental import pallas as pl
from jax.experimental.pallas import tpu as pltpu
from jax.sharding import PartitionSpec as P

MESH = pl.DeviceIdType.MESH
DC = 512
DR = 64
DN = 128
BIG = 1e30
EXP2_SCALE = (DN + DR) ** (-0.5) * 1.4426950408889634
NZ, NX = 4, 8
GROUP = 2 * NX
RING = 8
HEADS = 8
TOKENS = 128
PIECE = 16
LISTED = 16
LEVELS = 16
ROWS = HEADS * TOKENS
KEYS = LISTED * PIECE
LANES = 128
PARTS = 4
ROPE = 1
BATCH = 2
SHARD = tuple(24 if part == ROPE else 16 for part in range(PARTS))
MESSAGE = tuple(6 if part == ROPE else 4 for part in range(PARTS))
CHUNK = SHARD


def body(
    lists, cache, q_hbm, vup_hbm, seg_hbm, out, *scratch
):
    planes, sends, recvs, gats = (scratch[PARTS * i:PARTS * (i + 1)] for i in range(4))
    (
        q_in, vup, seg, want_in, comb, levels,
        qa, kcat, valid, m_ref, l_ref, acc,
        local_sem, level_sem, want_send, want_recv, plane_send, plane_recv,
        mess_send, mess_recv, ring_send, ring_recv,
    ) = scratch[4 * PARTS:]
    me = lax.axis_index("ctx")
    t = lax.axis_index("tp")
    z = me // GROUP
    spot = me % GROUP
    x = spot // 2
    core = spot % 2
    right = (t + 1) % RING
    left = (t + RING - 1) % RING
    above = ((z + 1) % NZ) * GROUP + spot
    below = ((z + NZ - 1) % NZ) * GROUP + spot

    def other(o):
        return ((x + o // 2) % NX) * 2 + (core + o % 2) % 2

    barrier = pltpu.get_barrier_semaphore()
    for peer in ((above, t), (below, t), (me, right), (me, left)):
        pl.semaphore_signal(barrier, inc=1, device_id=peer, device_id_type=MESH)

    def greet(o, carry):
        pl.semaphore_signal(
            barrier, inc=1, device_id=(z * GROUP + other(o), t), device_id_type=MESH
        )
        return carry

    lax.fori_loop(1, GROUP, greet, 0)

    locals_ = [
        pltpu.make_async_copy(q_hbm, q_in, local_sem.at[0]),
        pltpu.make_async_copy(vup_hbm, vup, local_sem.at[1]),
        pltpu.make_async_copy(seg_hbm, seg, local_sem.at[2]),
    ]
    for copy in locals_:
        copy.start()

    lane8 = lax.broadcasted_iota(jnp.int32, (8, LANES), 1)
    row = jnp.zeros((8, LANES), jnp.int32)
    for j in range(LISTED):
        entry = lists[0, j]
        row = jnp.where(lane8 == (entry & 63), entry >> 6, row)
    want_in[spot] = row

    for level in range(LEVELS):
        for part in range(PARTS):
            planes[part][z, level] = cache[level, :, part * LANES:(part + 1) * LANES]
        if level % 2 == 1:
            planes[ROPE][z, LEVELS + level // 2] = jnp.concatenate(
                [cache[level - 1, :, DC:], cache[level, :, DC:]], axis=1
            )

    def plane_copy(part, direction, step, arriving):
        whole = SHARD[part]
        hops = step if arriving else step - 1
        origin = (z + NZ - hops) % NZ if direction == 0 else (z + hops) % NZ
        start, count = (0, whole) if step == 1 else (direction * (whole // 2), whole // 2)
        piece = planes[part].at[origin, pl.ds(start, count)]
        return pltpu.make_async_remote_copy(
            src_ref=piece, dst_ref=piece,
            send_sem=plane_send.at[part, direction, step],
            recv_sem=plane_recv.at[part, direction, step],
            device_id=(above if direction == 0 else below, t), device_id_type=MESH,
        )

    pl.semaphore_wait(barrier, GROUP - 1 + 4)

    def want_copy(o):
        return pltpu.make_async_remote_copy(
            src_ref=want_in.at[spot], dst_ref=want_in.at[spot],
            send_sem=want_send.at[o], recv_sem=want_recv.at[spot],
            device_id=(z * GROUP + other(o), t), device_id_type=MESH,
        )

    def want_start(o, carry):
        want_copy(o).start()
        return carry

    def plane_open(part):
        for direction in range(2):
            plane_copy(part, direction, 1, False).start()

    plane_open(0)
    lax.fori_loop(1, GROUP, want_start, 0)
    plane_open(1)

    locals_[0].wait()
    for h in range(HEADS):
        rows = slice(h * TOKENS, (h + 1) * TOKENS)
        for i in range(4):
            qa[rows, i * LANES:(i + 1) * LANES] = q_in[h, i * LANES:(i + 1) * LANES, :].T
        rope = q_in[h, DC:DC + DR, :]
        qa[rows, DC:] = jnp.concatenate([rope, rope], axis=0).T

    def plane_pass(part):
        for direction in range(2):
            plane_copy(part, direction, 1, True).wait_recv()
            plane_copy(part, direction, 2, False).start()

    plane_pass(0)
    plane_open(2)

    def want_wait(o, carry):
        source = other(o)
        pltpu.make_async_remote_copy(
            src_ref=want_in.at[source], dst_ref=want_in.at[source],
            send_sem=want_send.at[o], recv_sem=want_recv.at[source],
            device_id=(z * GROUP + source, t), device_id_type=MESH,
        ).wait_recv()
        return carry

    lax.fori_loop(1, GROUP, want_wait, 0)
    for s in range(GROUP):
        comb[s:s + 1, :] = want_in[s, 0:1, :]
    to_scalar = pltpu.make_async_copy(comb, levels, level_sem)
    to_scalar.start()
    to_scalar.wait()

    def fill(part, dest, ref, slot):
        halves = []
        for plane in range(NZ):
            level = levels[dest, plane * GROUP + spot]
            ref[slot, plane] = planes[part][plane, level]
            if part == ROPE:
                tile = planes[part][plane, LEVELS + (level >> 1)]
                halves.append(jnp.where((level & 1) == 0, tile[:, :DR], tile[:, DR:]))
                if plane % 2 == 1:
                    ref[slot, NZ + plane // 2] = jnp.concatenate(halves, axis=1)
                    halves = []

    def message(part, o):
        return pltpu.make_async_remote_copy(
            src_ref=sends[part].at[o], dst_ref=recvs[part].at[spot],
            send_sem=mess_send.at[part, o], recv_sem=mess_recv.at[part, spot],
            device_id=(z * GROUP + other(o), t), device_id_type=MESH,
        )

    def plane_close(part):
        for direction in range(2):
            plane_copy(part, direction, 2, True).wait_recv()

        def send_one(o, carry):
            fill(part, other(o), sends[part], o)
            message(part, o).start()
            return carry

        lax.fori_loop(1, GROUP, send_one, 0)
        fill(part, spot, recvs[part], spot)

    locals_[2].wait()
    last = seg[pl.ds((LEVELS - 1) * NZ * GROUP + me, 1), :]
    query_seg = last[:, LANES - 1:LANES]
    for j in range(LISTED):
        place = (j % 2) * (LISTED // 2) + j // 2
        rollout = seg[pl.ds(lists[0, j], 1), :]
        valid[place:place + 1, :] = jnp.where(rollout == query_seg, 1.0, 0.0)

    m_ref[...] = jnp.full_like(m_ref, -BIG)
    l_ref[...] = jnp.zeros_like(l_ref)
    acc[...] = jnp.zeros_like(acc)

    def wait_messages(part):
        def one(o, carry):
            source = other(o)
            pltpu.make_async_remote_copy(
                src_ref=sends[part].at[o], dst_ref=recvs[part].at[source],
                send_sem=mess_send.at[part, o], recv_sem=mess_recv.at[part, source],
                device_id=(z * GROUP + source, t), device_id_type=MESH,
            ).wait_recv()
            return carry

        lax.fori_loop(1, GROUP, one, 0)

    def pick(part):
        halves = []
        for j in range(LISTED):
            place = (j % 2) * (LISTED // 2) + j // 2
            residue = lists[0, j] & 63
            plane = residue >> 4
            source = residue & 15
            gats[part][t, place] = recvs[part][source, plane]
            if part == ROPE:
                tile = recvs[part][source, NZ + (plane >> 1)]
                halves.append(jnp.where((plane & 1) == 0, tile[:, :DR], tile[:, DR:]))
                if j % 2 == 1:
                    gats[part][t, LISTED + j // 2] = jnp.concatenate(halves, axis=1)
                    halves = []

    def ring(part, direction, step, arriving):
        whole = CHUNK[part]
        hops = step if arriving else step - 1
        origin = (t + RING - hops) % RING if direction == 0 else (t + hops) % RING
        start, count = (0, whole) if step < 4 else (direction * (whole // 2), whole // 2)
        piece = gats[part].at[origin, pl.ds(start, count)]
        return pltpu.make_async_remote_copy(
            src_ref=piece, dst_ref=piece,
            send_sem=ring_send.at[part, direction, step],
            recv_sem=ring_recv.at[part, direction, step],
            device_id=(me, right if direction == 0 else left), device_id_type=MESH,
        )

    def ring_open(part):
        wait_messages(part)
        pick(part)
        for direction in range(2):
            ring(part, direction, 1, False).start()

    def ring_pass(part, step):
        for direction in range(2):
            ring(part, direction, step, True).wait_recv()
            if step < 4:
                ring(part, direction, step + 1, False).start()

    lane_r = lax.broadcasted_iota(jnp.int32, (KEYS // 2, LANES), 1)

    def attend(origins):
        count = len(origins) * KEYS
        biases = []
        for n, origin in enumerate(origins):
            first = slice(n * KEYS, n * KEYS + KEYS // 2)
            second = slice(n * KEYS + KEYS // 2, (n + 1) * KEYS)
            for part in range(PARTS):
                kcat[n * KEYS:(n + 1) * KEYS, part * LANES:(part + 1) * LANES] = gats[part][
                    origin, :LISTED
                ].reshape(KEYS, LANES)
            rope = gats[ROPE][origin, LISTED:].reshape(KEYS // 2, LANES)
            kcat[first, DC:] = jnp.where(lane_r < DR, rope, jnp.zeros_like(rope))
            kcat[second, DC:] = jnp.where(lane_r < DR, jnp.zeros_like(rope), rope)
            token = lax.broadcasted_iota(jnp.int32, (LANES, KEYS), 0)
            key = lax.broadcasted_iota(jnp.int32, (LANES, KEYS), 1)
            spread = jnp.where(token == origin * PIECE + key % PIECE, 1.0, 0.0).astype(jnp.bfloat16)
            seen = jnp.dot(
                valid[...].astype(jnp.bfloat16), spread, preferred_element_type=jnp.float32
            )
            place = lax.broadcasted_iota(jnp.int32, (LISTED, KEYS), 0)
            lane = lax.broadcasted_iota(jnp.int32, (LISTED, KEYS), 1)
            seen = jnp.sum(jnp.where(lane // PIECE == place, seen, 0.0), axis=0, keepdims=True)
            bias = jnp.broadcast_to((seen - 1.0) * BIG, (TOKENS, KEYS))
            query = lax.broadcasted_iota(jnp.int32, (TOKENS, KEYS), 0)
            column = lax.broadcasted_iota(jnp.int32, (TOKENS, KEYS), 1)
            later = (column < PIECE) & (origin * PIECE + column > query)
            biases.append(jnp.where(later, -BIG, bias))
        bias = jnp.concatenate(biases, axis=1) if len(origins) > 1 else biases[0]
        for g in range(HEADS // BATCH):
            rows = pl.ds(g * BATCH * TOKENS, BATCH * TOKENS)
            s = lax.dot_general(
                qa[rows, :], kcat[:count, :], (((1,), (1,)), ((), ())),
                preferred_element_type=jnp.float32,
            )
            s = (s.reshape(BATCH, TOKENS, count) + bias[None]).reshape(BATCH * TOKENS, count)
            m_old = m_ref[rows, :]
            m_new = jnp.maximum(m_old, jnp.max(s, axis=1, keepdims=True))
            alpha = jnp.exp2((m_old - m_new) * EXP2_SCALE)
            p = jnp.exp2((s - m_new[:, :1]) * EXP2_SCALE)
            l_new = l_ref[rows, :] * alpha
            for at in range(0, count, LANES):
                l_new = l_new + p[:, at:at + LANES]
            l_ref[rows, :] = l_new
            m_ref[rows, :] = m_new
            pv = jnp.dot(
                p.astype(jnp.bfloat16), kcat[:count, :DC], preferred_element_type=jnp.float32
            )
            acc[rows, :] = acc[rows, :] * alpha[:, :1] + pv

    plane_close(0)
    plane_pass(1)
    plane_open(3)
    plane_pass(2)
    plane_close(1)
    ring_open(0)
    plane_pass(3)
    plane_close(2)
    ring_pass(0, 1)
    plane_close(3)
    ring_open(1)
    ring_pass(0, 2)
    ring_open(2)
    ring_pass(1, 1)
    ring_open(3)
    ring_pass(0, 3)
    ring_pass(2, 1)
    attend([t])
    ring_pass(3, 1)
    ring_pass(1, 2)
    attend([left, right])
    ring_pass(2, 2)
    ring_pass(3, 2)
    ring_pass(1, 3)
    attend([(t + 6) % RING, (t + 2) % RING])
    ring_pass(2, 3)
    ring_pass(3, 3)
    attend([(t + 5) % RING, (t + 3) % RING])
    ring_pass(0, 4)
    ring_pass(1, 4)
    ring_pass(2, 4)
    ring_pass(3, 4)
    attend([(t + 4) % RING])

    locals_[1].wait()
    width = vup.shape[2]
    for h in range(HEADS):
        rows = pl.ds(h * TOKENS, TOKENS)
        total = jnp.sum(l_ref[rows, :], axis=1, keepdims=True)
        latent = (acc[rows, :] / total).astype(jnp.bfloat16)
        out[:, h * width:(h + 1) * width] = jnp.dot(
            latent, vup[h], preferred_element_type=jnp.float32
        ).astype(out.dtype)

    def sent(o, carry):
        want_copy(o).wait_send()
        for part in range(PARTS):
            message(part, o).wait_send()
        return carry

    lax.fori_loop(1, GROUP, sent, 0)
    for part in range(PARTS):
        for direction in range(2):
            for step in range(1, 3):
                plane_copy(part, direction, step, False).wait_send()
            for step in range(1, 5):
                ring(part, direction, step, False).wait_send()


def shards(queries, latent_cache, key_segments, block_lists, value_up):
    tokens, heads, width = queries.shape
    bf16, f32 = jnp.bfloat16, jnp.float32
    vmem = pl.BlockSpec(memory_space=pltpu.VMEM)
    anywhere = pl.BlockSpec(memory_space=pl.ANY)

    def tiles(outer, counts):
        return [pltpu.VMEM((outer, count, PIECE, LANES), bf16) for count in counts]

    sem = pltpu.SemaphoreType.DMA
    return pl.pallas_call(
        body,
        out_shape=jax.ShapeDtypeStruct((tokens, heads * value_up.shape[2]), bf16),
        in_specs=[pl.BlockSpec(memory_space=pltpu.SMEM), vmem, anywhere, anywhere, anywhere],
        out_specs=vmem,
        scratch_shapes=[
            *tiles(NZ, SHARD),
            *tiles(GROUP, MESSAGE),
            *tiles(GROUP, MESSAGE),
            *tiles(RING, CHUNK),
            pltpu.VMEM((heads, width, tokens), bf16),
            pltpu.VMEM(value_up.shape, bf16),
            pltpu.VMEM(key_segments.shape, jnp.int32),
            pltpu.VMEM((GROUP, 8, LANES), jnp.int32),
            pltpu.VMEM((GROUP, LANES), jnp.int32),
            pltpu.SMEM((GROUP, LANES), jnp.int32),
            pltpu.VMEM((ROWS, DC + LANES), bf16),
            pltpu.VMEM((2 * KEYS, DC + LANES), bf16),
            pltpu.VMEM((LISTED, LANES), f32),
            pltpu.VMEM((ROWS, LANES), f32),
            pltpu.VMEM((ROWS, LANES), f32),
            pltpu.VMEM((ROWS, DC), f32),
            sem((3,)),
            sem,
            sem((GROUP,)),
            sem((GROUP,)),
            sem((PARTS, 2, 3)),
            sem((PARTS, 2, 3)),
            sem((PARTS, GROUP)),
            sem((PARTS, GROUP)),
            sem((PARTS, 2, 5)),
            sem((PARTS, 2, 5)),
        ],
        compiler_params=pltpu.CompilerParams(
            collective_id=0, has_side_effects=True, vmem_limit_bytes=60 * 1024 * 1024
        ),
    )(block_lists, latent_cache, queries.transpose(1, 2, 0), value_up, key_segments)


def solution(mesh):
    return jax.shard_map(
        shards,
        mesh=mesh,
        in_specs=(
            P("ctx", "tp", None),
            P(None, ("ctx", "tp"), None),
            P(),
            P("ctx", None),
            P("tp", None, None),
        ),
        out_specs=P("ctx", "tp"),
        check_vma=False,
    )
```

```python
import jax
import jax.numpy as jnp
from jax import lax
from jax.experimental import pallas as pl
from jax.experimental.pallas import tpu as pltpu
from jax.sharding import PartitionSpec as P

MESH = pl.DeviceIdType.MESH
DC = 512
DR = 64
DN = 128
BIG = 1e30
EXP2_SCALE = (DN + DR) ** (-0.5) * 1.4426950408889634
NZ, NX = 4, 8
GROUP = 2 * NX
RING = 8
HEADS = 8
TOKENS = 128
PIECE = 16
LISTED = 16
LEVELS = 16
ROWS = HEADS * TOKENS
KEYS = LISTED * PIECE
LANES = 128
PARTS = 4
ROPE = 1
BATCH = 2
SHARD = tuple(24 if part == ROPE else 16 for part in range(PARTS))
MESSAGE = tuple(6 if part == ROPE else 4 for part in range(PARTS))
CHUNK = SHARD


def body(
    lists, cache, q_hbm, vup_hbm, seg_hbm, out, *scratch
):
    planes, sends, recvs, gats = (scratch[PARTS * i:PARTS * (i + 1)] for i in range(4))
    (
        q_in, vup, seg, want_in, comb, levels,
        qa, kcat, valid, m_ref, l_ref, acc,
        local_sem, level_sem, want_send, want_recv, plane_send, plane_recv,
        mess_send, mess_recv, ring_send, ring_recv,
    ) = scratch[4 * PARTS:]
    me = lax.axis_index("ctx")
    t = lax.axis_index("tp")
    z = me // GROUP
    spot = me % GROUP
    x = spot // 2
    core = spot % 2
    right = (t + 1) % RING
    left = (t + RING - 1) % RING
    above = ((z + 1) % NZ) * GROUP + spot
    below = ((z + NZ - 1) % NZ) * GROUP + spot

    def other(o):
        return ((x + o // 2) % NX) * 2 + (core + o % 2) % 2

    barrier = pltpu.get_barrier_semaphore()
    for peer in ((above, t), (below, t), (me, right), (me, left)):
        pl.semaphore_signal(barrier, inc=1, device_id=peer, device_id_type=MESH)

    def greet(o, carry):
        pl.semaphore_signal(
            barrier, inc=1, device_id=(z * GROUP + other(o), t), device_id_type=MESH
        )
        return carry

    lax.fori_loop(1, GROUP, greet, 0)

    locals_ = [
        pltpu.make_async_copy(q_hbm, q_in, local_sem.at[0]),
        pltpu.make_async_copy(vup_hbm, vup, local_sem.at[1]),
        pltpu.make_async_copy(seg_hbm, seg, local_sem.at[2]),
    ]
    for copy in locals_:
        copy.start()

    lane8 = lax.broadcasted_iota(jnp.int32, (8, LANES), 1)
    row = jnp.zeros((8, LANES), jnp.int32)
    for j in range(LISTED):
        entry = lists[0, j]
        row = jnp.where(lane8 == (entry & 63), entry >> 6, row)
    want_in[spot] = row

    for level in range(LEVELS):
        for part in range(PARTS):
            planes[part][z, level] = cache[level, :, part * LANES:(part + 1) * LANES]
        if level % 2 == 1:
            planes[ROPE][z, LEVELS + level // 2] = jnp.concatenate(
                [cache[level - 1, :, DC:], cache[level, :, DC:]], axis=1
            )

    def plane_copy(part, direction, step, arriving):
        whole = SHARD[part]
        hops = step if arriving else step - 1
        origin = (z + NZ - hops) % NZ if direction == 0 else (z + hops) % NZ
        start, count = (0, whole) if step == 1 else (direction * (whole // 2), whole // 2)
        piece = planes[part].at[origin, pl.ds(start, count)]
        return pltpu.make_async_remote_copy(
            src_ref=piece, dst_ref=piece,
            send_sem=plane_send.at[part, direction, step],
            recv_sem=plane_recv.at[part, direction, step],
            device_id=(above if direction == 0 else below, t), device_id_type=MESH,
        )

    pl.semaphore_wait(barrier, GROUP - 1 + 4)

    def want_copy(o):
        return pltpu.make_async_remote_copy(
            src_ref=want_in.at[spot], dst_ref=want_in.at[spot],
            send_sem=want_send.at[o], recv_sem=want_recv.at[spot],
            device_id=(z * GROUP + other(o), t), device_id_type=MESH,
        )

    def want_start(o, carry):
        want_copy(o).start()
        return carry

    def plane_open(part):
        for direction in range(2):
            plane_copy(part, direction, 1, False).start()

    plane_open(0)
    lax.fori_loop(1, GROUP, want_start, 0)
    plane_open(1)

    locals_[0].wait()
    for h in range(HEADS):
        rows = slice(h * TOKENS, (h + 1) * TOKENS)
        for i in range(4):
            qa[rows, i * LANES:(i + 1) * LANES] = q_in[h, i * LANES:(i + 1) * LANES, :].T
        rope = q_in[h, DC:DC + DR, :]
        qa[rows, DC:] = jnp.concatenate([rope, rope], axis=0).T

    def plane_pass(part):
        for direction in range(2):
            plane_copy(part, direction, 1, True).wait_recv()
            plane_copy(part, direction, 2, False).start()

    plane_pass(0)
    plane_open(2)

    def want_wait(o, carry):
        source = other(o)
        pltpu.make_async_remote_copy(
            src_ref=want_in.at[source], dst_ref=want_in.at[source],
            send_sem=want_send.at[o], recv_sem=want_recv.at[source],
            device_id=(z * GROUP + source, t), device_id_type=MESH,
        ).wait_recv()
        return carry

    lax.fori_loop(1, GROUP, want_wait, 0)
    for s in range(GROUP):
        comb[s:s + 1, :] = want_in[s, 0:1, :]
    to_scalar = pltpu.make_async_copy(comb, levels, level_sem)
    to_scalar.start()
    to_scalar.wait()

    def fill(part, dest, ref, slot):
        halves = []
        for plane in range(NZ):
            level = levels[dest, plane * GROUP + spot]
            ref[slot, plane] = planes[part][plane, level]
            if part == ROPE:
                tile = planes[part][plane, LEVELS + (level >> 1)]
                halves.append(jnp.where((level & 1) == 0, tile[:, :DR], tile[:, DR:]))
                if plane % 2 == 1:
                    ref[slot, NZ + plane // 2] = jnp.concatenate(halves, axis=1)
                    halves = []

    def message(part, o):
        return pltpu.make_async_remote_copy(
            src_ref=sends[part].at[o], dst_ref=recvs[part].at[spot],
            send_sem=mess_send.at[part, o], recv_sem=mess_recv.at[part, spot],
            device_id=(z * GROUP + other(o), t), device_id_type=MESH,
        )

    def plane_close(part):
        for direction in range(2):
            plane_copy(part, direction, 2, True).wait_recv()

        def send_one(o, carry):
            fill(part, other(o), sends[part], o)
            message(part, o).start()
            return carry

        lax.fori_loop(1, GROUP, send_one, 0)
        fill(part, spot, recvs[part], spot)

    locals_[2].wait()
    last = seg[pl.ds((LEVELS - 1) * NZ * GROUP + me, 1), :]
    query_seg = last[:, LANES - 1:LANES]
    for j in range(LISTED):
        place = (j % 2) * (LISTED // 2) + j // 2
        rollout = seg[pl.ds(lists[0, j], 1), :]
        valid[place:place + 1, :] = jnp.where(rollout == query_seg, 1.0, 0.0)

    m_ref[...] = jnp.full_like(m_ref, -BIG)
    l_ref[...] = jnp.zeros_like(l_ref)
    acc[...] = jnp.zeros_like(acc)

    def wait_messages(part):
        def one(o, carry):
            source = other(o)
            pltpu.make_async_remote_copy(
                src_ref=sends[part].at[o], dst_ref=recvs[part].at[source],
                send_sem=mess_send.at[part, o], recv_sem=mess_recv.at[part, source],
                device_id=(z * GROUP + source, t), device_id_type=MESH,
            ).wait_recv()
            return carry

        lax.fori_loop(1, GROUP, one, 0)

    def pick(part):
        halves = []
        for j in range(LISTED):
            place = (j % 2) * (LISTED // 2) + j // 2
            residue = lists[0, j] & 63
            plane = residue >> 4
            source = residue & 15
            gats[part][t, place] = recvs[part][source, plane]
            if part == ROPE:
                tile = recvs[part][source, NZ + (plane >> 1)]
                halves.append(jnp.where((plane & 1) == 0, tile[:, :DR], tile[:, DR:]))
                if j % 2 == 1:
                    gats[part][t, LISTED + j // 2] = jnp.concatenate(halves, axis=1)
                    halves = []

    def ring(part, direction, step, arriving):
        whole = CHUNK[part]
        hops = step if arriving else step - 1
        origin = (t + RING - hops) % RING if direction == 0 else (t + hops) % RING
        start, count = (0, whole) if step < 4 else (direction * (whole // 2), whole // 2)
        piece = gats[part].at[origin, pl.ds(start, count)]
        return pltpu.make_async_remote_copy(
            src_ref=piece, dst_ref=piece,
            send_sem=ring_send.at[part, direction, step],
            recv_sem=ring_recv.at[part, direction, step],
            device_id=(me, right if direction == 0 else left), device_id_type=MESH,
        )

    def ring_open(part):
        wait_messages(part)
        pick(part)
        for direction in range(2):
            ring(part, direction, 1, False).start()

    def ring_pass(part, step):
        for direction in range(2):
            ring(part, direction, step, True).wait_recv()
            if step < 4:
                ring(part, direction, step + 1, False).start()

    lane_r = lax.broadcasted_iota(jnp.int32, (KEYS // 2, LANES), 1)

    def attend(origins):
        count = len(origins) * KEYS
        biases = []
        for n, origin in enumerate(origins):
            first = slice(n * KEYS, n * KEYS + KEYS // 2)
            second = slice(n * KEYS + KEYS // 2, (n + 1) * KEYS)
            for part in range(PARTS):
                kcat[n * KEYS:(n + 1) * KEYS, part * LANES:(part + 1) * LANES] = gats[part][
                    origin, :LISTED
                ].reshape(KEYS, LANES)
            rope = gats[ROPE][origin, LISTED:].reshape(KEYS // 2, LANES)
            kcat[first, DC:] = jnp.where(lane_r < DR, rope, jnp.zeros_like(rope))
            kcat[second, DC:] = jnp.where(lane_r < DR, jnp.zeros_like(rope), rope)
            token = lax.broadcasted_iota(jnp.int32, (LANES, KEYS), 0)
            key = lax.broadcasted_iota(jnp.int32, (LANES, KEYS), 1)
            spread = jnp.where(token == origin * PIECE + key % PIECE, 1.0, 0.0).astype(jnp.bfloat16)
            seen = jnp.dot(
                valid[...].astype(jnp.bfloat16), spread, preferred_element_type=jnp.float32
            )
            place = lax.broadcasted_iota(jnp.int32, (LISTED, KEYS), 0)
            lane = lax.broadcasted_iota(jnp.int32, (LISTED, KEYS), 1)
            seen = jnp.sum(jnp.where(lane // PIECE == place, seen, 0.0), axis=0, keepdims=True)
            bias = jnp.broadcast_to((seen - 1.0) * BIG, (TOKENS, KEYS))
            query = lax.broadcasted_iota(jnp.int32, (TOKENS, KEYS), 0)
            column = lax.broadcasted_iota(jnp.int32, (TOKENS, KEYS), 1)
            later = (column < PIECE) & (origin * PIECE + column > query)
            biases.append(jnp.where(later, -BIG, bias))
        bias = jnp.concatenate(biases, axis=1) if len(origins) > 1 else biases[0]
        for g in range(HEADS // BATCH):
            rows = pl.ds(g * BATCH * TOKENS, BATCH * TOKENS)
            s = lax.dot_general(
                qa[rows, :], kcat[:count, :], (((1,), (1,)), ((), ())),
                preferred_element_type=jnp.float32,
            )
            s = (s.reshape(BATCH, TOKENS, count) + bias[None]).reshape(BATCH * TOKENS, count)
            m_old = m_ref[rows, :]
            m_new = jnp.maximum(m_old, jnp.max(s, axis=1, keepdims=True))
            alpha = jnp.exp2((m_old - m_new) * EXP2_SCALE)
            p = jnp.exp2((s - m_new[:, :1]) * EXP2_SCALE)
            l_new = l_ref[rows, :] * alpha
            for at in range(0, count, LANES):
                l_new = l_new + p[:, at:at + LANES]
            l_ref[rows, :] = l_new
            m_ref[rows, :] = m_new
            pv = jnp.dot(
                p.astype(jnp.bfloat16), kcat[:count, :DC], preferred_element_type=jnp.float32
            )
            acc[rows, :] = acc[rows, :] * alpha[:, :1] + pv

    plane_close(0)
    plane_pass(1)
    plane_open(3)
    plane_pass(2)
    ring_open(0)
    plane_close(1)
    plane_pass(3)
    ring_pass(0, 1)
    plane_close(2)
    ring_pass(0, 2)
    plane_close(3)
    ring_open(1)
    ring_pass(0, 3)
    ring_open(2)
    ring_pass(1, 1)
    ring_open(3)
    ring_pass(2, 1)
    attend([t])
    ring_pass(3, 1)
    ring_pass(1, 2)
    attend([left, right])
    ring_pass(2, 2)
    ring_pass(3, 2)
    ring_pass(1, 3)
    attend([(t + 6) % RING, (t + 2) % RING])
    ring_pass(2, 3)
    ring_pass(3, 3)
    attend([(t + 5) % RING, (t + 3) % RING])
    ring_pass(0, 4)
    ring_pass(1, 4)
    ring_pass(2, 4)
    ring_pass(3, 4)
    attend([(t + 4) % RING])

    locals_[1].wait()
    width = vup.shape[2]
    for h in range(HEADS):
        rows = pl.ds(h * TOKENS, TOKENS)
        total = jnp.sum(l_ref[rows, :], axis=1, keepdims=True)
        latent = (acc[rows, :] / total).astype(jnp.bfloat16)
        out[:, h * width:(h + 1) * width] = jnp.dot(
            latent, vup[h], preferred_element_type=jnp.float32
        ).astype(out.dtype)

    def sent(o, carry):
        want_copy(o).wait_send()
        for part in range(PARTS):
            message(part, o).wait_send()
        return carry

    lax.fori_loop(1, GROUP, sent, 0)
    for part in range(PARTS):
        for direction in range(2):
            for step in range(1, 3):
                plane_copy(part, direction, step, False).wait_send()
            for step in range(1, 5):
                ring(part, direction, step, False).wait_send()


def shards(queries, latent_cache, key_segments, block_lists, value_up):
    tokens, heads, width = queries.shape
    bf16, f32 = jnp.bfloat16, jnp.float32
    vmem = pl.BlockSpec(memory_space=pltpu.VMEM)
    anywhere = pl.BlockSpec(memory_space=pl.ANY)

    def tiles(outer, counts):
        return [pltpu.VMEM((outer, count, PIECE, LANES), bf16) for count in counts]

    sem = pltpu.SemaphoreType.DMA
    return pl.pallas_call(
        body,
        out_shape=jax.ShapeDtypeStruct((tokens, heads * value_up.shape[2]), bf16),
        in_specs=[pl.BlockSpec(memory_space=pltpu.SMEM), vmem, anywhere, anywhere, anywhere],
        out_specs=vmem,
        scratch_shapes=[
            *tiles(NZ, SHARD),
            *tiles(GROUP, MESSAGE),
            *tiles(GROUP, MESSAGE),
            *tiles(RING, CHUNK),
            pltpu.VMEM((heads, width, tokens), bf16),
            pltpu.VMEM(value_up.shape, bf16),
            pltpu.VMEM(key_segments.shape, jnp.int32),
            pltpu.VMEM((GROUP, 8, LANES), jnp.int32),
            pltpu.VMEM((GROUP, LANES), jnp.int32),
            pltpu.SMEM((GROUP, LANES), jnp.int32),
            pltpu.VMEM((ROWS, DC + LANES), bf16),
            pltpu.VMEM((2 * KEYS, DC + LANES), bf16),
            pltpu.VMEM((LISTED, LANES), f32),
            pltpu.VMEM((ROWS, LANES), f32),
            pltpu.VMEM((ROWS, LANES), f32),
            pltpu.VMEM((ROWS, DC), f32),
            sem((3,)),
            sem,
            sem((GROUP,)),
            sem((GROUP,)),
            sem((PARTS, 2, 3)),
            sem((PARTS, 2, 3)),
            sem((PARTS, GROUP)),
            sem((PARTS, GROUP)),
            sem((PARTS, 2, 5)),
            sem((PARTS, 2, 5)),
        ],
        compiler_params=pltpu.CompilerParams(
            collective_id=0, has_side_effects=True, vmem_limit_bytes=60 * 1024 * 1024
        ),
    )(block_lists, latent_cache, queries.transpose(1, 2, 0), value_up, key_segments)


def solution(mesh):
    return jax.shard_map(
        shards,
        mesh=mesh,
        in_specs=(
            P("ctx", "tp", None),
            P(None, ("ctx", "tp"), None),
            P(),
            P("ctx", None),
            P("tp", None, None),
        ),
        out_specs=P("ctx", "tp"),
        check_vma=False,
    )
```

```python
import jax
import jax.numpy as jnp
from jax import lax
from jax.experimental import pallas as pl
from jax.experimental.pallas import tpu as pltpu
from jax.sharding import PartitionSpec as P

MESH = pl.DeviceIdType.MESH
DC = 512
DR = 64
DN = 128
BIG = 1e30
EXP2_SCALE = (DN + DR) ** (-0.5) * 1.4426950408889634
NZ, NX = 4, 8
GROUP = 2 * NX
RING = 8
HEADS = 8
TOKENS = 128
PIECE = 16
LISTED = 16
LEVELS = 16
ROWS = HEADS * TOKENS
KEYS = LISTED * PIECE
LANES = 128
PARTS = 4
ROPE = 1
BATCH = 2
SHARD = tuple(24 if part == ROPE else 16 for part in range(PARTS))
MESSAGE = tuple(6 if part == ROPE else 4 for part in range(PARTS))
CHUNK = SHARD


def body(
    lists, cache, q_hbm, vup_hbm, seg_hbm, out, *scratch
):
    planes, sends, recvs, gats = (scratch[PARTS * i:PARTS * (i + 1)] for i in range(4))
    (
        q_in, vup, seg, want_in, comb, levels,
        qa, kcat, valid, m_ref, l_ref, acc,
        local_sem, level_sem, want_send, want_recv, plane_send, plane_recv,
        mess_send, mess_recv, ring_send, ring_recv,
    ) = scratch[4 * PARTS:]
    me = lax.axis_index("ctx")
    t = lax.axis_index("tp")
    z = me // GROUP
    spot = me % GROUP
    x = spot // 2
    core = spot % 2
    right = (t + 1) % RING
    left = (t + RING - 1) % RING
    above = ((z + 1) % NZ) * GROUP + spot
    below = ((z + NZ - 1) % NZ) * GROUP + spot

    def other(o):
        return ((x + o // 2) % NX) * 2 + (core + o % 2) % 2

    barrier = pltpu.get_barrier_semaphore()
    for peer in ((above, t), (below, t), (me, right), (me, left)):
        pl.semaphore_signal(barrier, inc=1, device_id=peer, device_id_type=MESH)

    def greet(o, carry):
        pl.semaphore_signal(
            barrier, inc=1, device_id=(z * GROUP + other(o), t), device_id_type=MESH
        )
        return carry

    lax.fori_loop(1, GROUP, greet, 0)

    locals_ = [
        pltpu.make_async_copy(q_hbm, q_in, local_sem.at[0]),
        pltpu.make_async_copy(vup_hbm, vup, local_sem.at[1]),
        pltpu.make_async_copy(seg_hbm, seg, local_sem.at[2]),
    ]
    for copy in locals_:
        copy.start()

    lane8 = lax.broadcasted_iota(jnp.int32, (8, LANES), 1)
    row = jnp.zeros((8, LANES), jnp.int32)
    for j in range(LISTED):
        entry = lists[0, j]
        row = jnp.where(lane8 == (entry & 63), entry >> 6, row)
    want_in[spot] = row

    for level in range(LEVELS):
        for part in range(PARTS):
            planes[part][z, level] = cache[level, :, part * LANES:(part + 1) * LANES]
        if level % 2 == 1:
            planes[ROPE][z, LEVELS + level // 2] = jnp.concatenate(
                [cache[level - 1, :, DC:], cache[level, :, DC:]], axis=1
            )

    def plane_copy(part, direction, step, arriving):
        whole = SHARD[part]
        hops = step if arriving else step - 1
        origin = (z + NZ - hops) % NZ if direction == 0 else (z + hops) % NZ
        start, count = (0, whole) if step == 1 else (direction * (whole // 2), whole // 2)
        piece = planes[part].at[origin, pl.ds(start, count)]
        return pltpu.make_async_remote_copy(
            src_ref=piece, dst_ref=piece,
            send_sem=plane_send.at[part, direction, step],
            recv_sem=plane_recv.at[part, direction, step],
            device_id=(above if direction == 0 else below, t), device_id_type=MESH,
        )

    pl.semaphore_wait(barrier, GROUP - 1 + 4)

    def want_copy(o):
        return pltpu.make_async_remote_copy(
            src_ref=want_in.at[spot], dst_ref=want_in.at[spot],
            send_sem=want_send.at[o], recv_sem=want_recv.at[spot],
            device_id=(z * GROUP + other(o), t), device_id_type=MESH,
        )

    def want_start(o, carry):
        want_copy(o).start()
        return carry

    def plane_open(part):
        for direction in range(2):
            plane_copy(part, direction, 1, False).start()

    plane_open(0)
    lax.fori_loop(1, GROUP, want_start, 0)
    plane_open(1)

    locals_[0].wait()
    for h in range(HEADS):
        rows = slice(h * TOKENS, (h + 1) * TOKENS)
        for i in range(4):
            qa[rows, i * LANES:(i + 1) * LANES] = q_in[h, i * LANES:(i + 1) * LANES, :].T
        rope = q_in[h, DC:DC + DR, :]
        qa[rows, DC:] = jnp.concatenate([rope, rope], axis=0).T

    def plane_pass(part):
        for direction in range(2):
            plane_copy(part, direction, 1, True).wait_recv()
            plane_copy(part, direction, 2, False).start()

    plane_pass(0)
    plane_open(2)

    def want_wait(o, carry):
        source = other(o)
        pltpu.make_async_remote_copy(
            src_ref=want_in.at[source], dst_ref=want_in.at[source],
            send_sem=want_send.at[o], recv_sem=want_recv.at[source],
            device_id=(z * GROUP + source, t), device_id_type=MESH,
        ).wait_recv()
        return carry

    lax.fori_loop(1, GROUP, want_wait, 0)
    for s in range(GROUP):
        comb[s:s + 1, :] = want_in[s, 0:1, :]
    to_scalar = pltpu.make_async_copy(comb, levels, level_sem)
    to_scalar.start()
    to_scalar.wait()

    def fill(part, dest, ref, slot):
        halves = []
        for plane in range(NZ):
            level = levels[dest, plane * GROUP + spot]
            ref[slot, plane] = planes[part][plane, level]
            if part == ROPE:
                tile = planes[part][plane, LEVELS + (level >> 1)]
                halves.append(jnp.where((level & 1) == 0, tile[:, :DR], tile[:, DR:]))
                if plane % 2 == 1:
                    ref[slot, NZ + plane // 2] = jnp.concatenate(halves, axis=1)
                    halves = []

    def message(part, o):
        return pltpu.make_async_remote_copy(
            src_ref=sends[part].at[o], dst_ref=recvs[part].at[spot],
            send_sem=mess_send.at[part, o], recv_sem=mess_recv.at[part, spot],
            device_id=(z * GROUP + other(o), t), device_id_type=MESH,
        )

    def plane_close(part):
        for direction in range(2):
            plane_copy(part, direction, 2, True).wait_recv()

        def send_one(o, carry):
            fill(part, other(o), sends[part], o)
            message(part, o).start()
            return carry

        lax.fori_loop(1, GROUP, send_one, 0)
        fill(part, spot, recvs[part], spot)

    locals_[2].wait()
    last = seg[pl.ds((LEVELS - 1) * NZ * GROUP + me, 1), :]
    query_seg = last[:, LANES - 1:LANES]
    for j in range(LISTED):
        place = (j % 2) * (LISTED // 2) + j // 2
        rollout = seg[pl.ds(lists[0, j], 1), :]
        valid[place:place + 1, :] = jnp.where(rollout == query_seg, 1.0, 0.0)

    m_ref[...] = jnp.full_like(m_ref, -BIG)
    l_ref[...] = jnp.zeros_like(l_ref)
    acc[...] = jnp.zeros_like(acc)

    def wait_messages(part):
        def one(o, carry):
            source = other(o)
            pltpu.make_async_remote_copy(
                src_ref=sends[part].at[o], dst_ref=recvs[part].at[source],
                send_sem=mess_send.at[part, o], recv_sem=mess_recv.at[part, source],
                device_id=(z * GROUP + source, t), device_id_type=MESH,
            ).wait_recv()
            return carry

        lax.fori_loop(1, GROUP, one, 0)

    def pick(part):
        halves = []
        for j in range(LISTED):
            place = (j % 2) * (LISTED // 2) + j // 2
            residue = lists[0, j] & 63
            plane = residue >> 4
            source = residue & 15
            gats[part][t, place] = recvs[part][source, plane]
            if part == ROPE:
                tile = recvs[part][source, NZ + (plane >> 1)]
                halves.append(jnp.where((plane & 1) == 0, tile[:, :DR], tile[:, DR:]))
                if j % 2 == 1:
                    gats[part][t, LISTED + j // 2] = jnp.concatenate(halves, axis=1)
                    halves = []

    def ring(part, direction, step, arriving):
        whole = CHUNK[part]
        hops = step if arriving else step - 1
        origin = (t + RING - hops) % RING if direction == 0 else (t + hops) % RING
        start, count = (0, whole) if step < 4 else (direction * (whole // 2), whole // 2)
        piece = gats[part].at[origin, pl.ds(start, count)]
        return pltpu.make_async_remote_copy(
            src_ref=piece, dst_ref=piece,
            send_sem=ring_send.at[part, direction, step],
            recv_sem=ring_recv.at[part, direction, step],
            device_id=(me, right if direction == 0 else left), device_id_type=MESH,
        )

    def ring_open(part):
        wait_messages(part)
        pick(part)
        for direction in range(2):
            ring(part, direction, 1, False).start()

    def ring_pass(part, step):
        for direction in range(2):
            ring(part, direction, step, True).wait_recv()
            if step < 4:
                ring(part, direction, step + 1, False).start()

    lane_r = lax.broadcasted_iota(jnp.int32, (KEYS // 2, LANES), 1)

    def attend(origins):
        count = len(origins) * KEYS
        biases = []
        for n, origin in enumerate(origins):
            first = slice(n * KEYS, n * KEYS + KEYS // 2)
            second = slice(n * KEYS + KEYS // 2, (n + 1) * KEYS)
            for part in range(PARTS):
                kcat[n * KEYS:(n + 1) * KEYS, part * LANES:(part + 1) * LANES] = gats[part][
                    origin, :LISTED
                ].reshape(KEYS, LANES)
            rope = gats[ROPE][origin, LISTED:].reshape(KEYS // 2, LANES)
            kcat[first, DC:] = jnp.where(lane_r < DR, rope, jnp.zeros_like(rope))
            kcat[second, DC:] = jnp.where(lane_r < DR, jnp.zeros_like(rope), rope)
            token = lax.broadcasted_iota(jnp.int32, (LANES, KEYS), 0)
            key = lax.broadcasted_iota(jnp.int32, (LANES, KEYS), 1)
            spread = jnp.where(token == origin * PIECE + key % PIECE, 1.0, 0.0).astype(jnp.bfloat16)
            seen = jnp.dot(
                valid[...].astype(jnp.bfloat16), spread, preferred_element_type=jnp.float32
            )
            place = lax.broadcasted_iota(jnp.int32, (LISTED, KEYS), 0)
            lane = lax.broadcasted_iota(jnp.int32, (LISTED, KEYS), 1)
            seen = jnp.sum(jnp.where(lane // PIECE == place, seen, 0.0), axis=0, keepdims=True)
            bias = jnp.broadcast_to((seen - 1.0) * BIG, (TOKENS, KEYS))
            query = lax.broadcasted_iota(jnp.int32, (TOKENS, KEYS), 0)
            column = lax.broadcasted_iota(jnp.int32, (TOKENS, KEYS), 1)
            later = (column < PIECE) & (origin * PIECE + column > query)
            biases.append(jnp.where(later, -BIG, bias))
        bias = jnp.concatenate(biases, axis=1) if len(origins) > 1 else biases[0]
        for g in range(HEADS // BATCH):
            rows = pl.ds(g * BATCH * TOKENS, BATCH * TOKENS)
            s = lax.dot_general(
                qa[rows, :], kcat[:count, :], (((1,), (1,)), ((), ())),
                preferred_element_type=jnp.float32,
            )
            s = (s.reshape(BATCH, TOKENS, count) + bias[None]).reshape(BATCH * TOKENS, count)
            m_old = m_ref[rows, :]
            m_new = jnp.maximum(m_old, jnp.max(s, axis=1, keepdims=True))
            alpha = jnp.exp2((m_old - m_new) * EXP2_SCALE)
            p = jnp.exp2((s - m_new[:, :1]) * EXP2_SCALE)
            l_new = l_ref[rows, :] * alpha
            for at in range(0, count, LANES):
                l_new = l_new + p[:, at:at + LANES]
            l_ref[rows, :] = l_new
            m_ref[rows, :] = m_new
            pv = jnp.dot(
                p.astype(jnp.bfloat16), kcat[:count, :DC], preferred_element_type=jnp.float32
            )
            acc[rows, :] = acc[rows, :] * alpha[:, :1] + pv

    plane_close(0)
    plane_pass(1)
    plane_open(3)
    plane_pass(2)
    plane_close(1)
    ring_open(0)
    plane_pass(3)
    plane_close(2)
    ring_pass(0, 1)
    plane_close(3)
    ring_open(1)
    ring_pass(0, 2)
    ring_open(2)
    ring_pass(1, 1)
    ring_open(3)
    ring_pass(0, 3)
    ring_pass(2, 1)
    attend([t])
    ring_pass(3, 1)
    ring_pass(1, 2)
    ring_pass(2, 2)
    attend([left, right])
    ring_pass(3, 2)
    ring_pass(1, 3)
    ring_pass(2, 3)
    attend([(t + 6) % RING, (t + 2) % RING])
    ring_pass(3, 3)
    attend([(t + 5) % RING, (t + 3) % RING])
    ring_pass(0, 4)
    ring_pass(1, 4)
    ring_pass(2, 4)
    ring_pass(3, 4)
    attend([(t + 4) % RING])

    locals_[1].wait()
    width = vup.shape[2]
    for h in range(HEADS):
        rows = pl.ds(h * TOKENS, TOKENS)
        total = jnp.sum(l_ref[rows, :], axis=1, keepdims=True)
        latent = (acc[rows, :] / total).astype(jnp.bfloat16)
        out[:, h * width:(h + 1) * width] = jnp.dot(
            latent, vup[h], preferred_element_type=jnp.float32
        ).astype(out.dtype)

    def sent(o, carry):
        want_copy(o).wait_send()
        for part in range(PARTS):
            message(part, o).wait_send()
        return carry

    lax.fori_loop(1, GROUP, sent, 0)
    for part in range(PARTS):
        for direction in range(2):
            for step in range(1, 3):
                plane_copy(part, direction, step, False).wait_send()
            for step in range(1, 5):
                ring(part, direction, step, False).wait_send()


def shards(queries, latent_cache, key_segments, block_lists, value_up):
    tokens, heads, width = queries.shape
    bf16, f32 = jnp.bfloat16, jnp.float32
    vmem = pl.BlockSpec(memory_space=pltpu.VMEM)
    anywhere = pl.BlockSpec(memory_space=pl.ANY)

    def tiles(outer, counts):
        return [pltpu.VMEM((outer, count, PIECE, LANES), bf16) for count in counts]

    sem = pltpu.SemaphoreType.DMA
    return pl.pallas_call(
        body,
        out_shape=jax.ShapeDtypeStruct((tokens, heads * value_up.shape[2]), bf16),
        in_specs=[pl.BlockSpec(memory_space=pltpu.SMEM), vmem, anywhere, anywhere, anywhere],
        out_specs=vmem,
        scratch_shapes=[
            *tiles(NZ, SHARD),
            *tiles(GROUP, MESSAGE),
            *tiles(GROUP, MESSAGE),
            *tiles(RING, CHUNK),
            pltpu.VMEM((heads, width, tokens), bf16),
            pltpu.VMEM(value_up.shape, bf16),
            pltpu.VMEM(key_segments.shape, jnp.int32),
            pltpu.VMEM((GROUP, 8, LANES), jnp.int32),
            pltpu.VMEM((GROUP, LANES), jnp.int32),
            pltpu.SMEM((GROUP, LANES), jnp.int32),
            pltpu.VMEM((ROWS, DC + LANES), bf16),
            pltpu.VMEM((2 * KEYS, DC + LANES), bf16),
            pltpu.VMEM((LISTED, LANES), f32),
            pltpu.VMEM((ROWS, LANES), f32),
            pltpu.VMEM((ROWS, LANES), f32),
            pltpu.VMEM((ROWS, DC), f32),
            sem((3,)),
            sem,
            sem((GROUP,)),
            sem((GROUP,)),
            sem((PARTS, 2, 3)),
            sem((PARTS, 2, 3)),
            sem((PARTS, GROUP)),
            sem((PARTS, GROUP)),
            sem((PARTS, 2, 5)),
            sem((PARTS, 2, 5)),
        ],
        compiler_params=pltpu.CompilerParams(
            collective_id=0, has_side_effects=True, vmem_limit_bytes=60 * 1024 * 1024
        ),
    )(block_lists, latent_cache, queries.transpose(1, 2, 0), value_up, key_segments)


def solution(mesh):
    return jax.shard_map(
        shards,
        mesh=mesh,
        in_specs=(
            P("ctx", "tp", None),
            P(None, ("ctx", "tp"), None),
            P(),
            P("ctx", None),
            P("tp", None, None),
        ),
        out_specs=P("ctx", "tp"),
        check_vma=False,
    )
```
